128 devices in a mesh: dp: 2 (over y_hi), expert: 64 (over z, y_lo, x, core).
Axes of the slice: x: 4, y: 4 (y_hi: 2, y_lo: 2; y = y_hi * 2 + y_lo), z: 4, core: 2. Of those that a mesh axis runs over, the one named last changes fastest.
Arguments:
- tokens: bfloat16 [2, 8192, 3584], P(None, ('dp', 'expert')), may hold values from -6 to 6
- expert_ids: int32 [2, 8192, 8], P(None, ('dp', 'expert')), may hold values from 0 to 127, all different within a row; in each aligned block of 64 rows (0 to 63, 64 to 127, ..., all dimensions but the last counted through in order) at most 5 rows name the same one
- gate_weights: float32 [2, 8192, 8], P(None, ('dp', 'expert')), may hold values from 0.05 to 0.6
- slot_expert: int32 [128], replicated, may hold values from 0 to 127, each once
- w_gate: bfloat16 [128, 3584, 1024], P(('dp', 'expert')), may hold values from -0.09375 to 0.09375
- w_up: bfloat16 [128, 3584, 1024], P(('dp', 'expert')), may hold values from -0.09375 to 0.09375
- w_down: bfloat16 [128, 1024, 3584], P(('dp', 'expert')), may hold values from -0.1875 to 0.1875
Outputs:
- mixed: bfloat16 [2, 8192, 3584], P(None, ('dp', 'expert'))
The draws below stay inside these ranges and needn't reach their ends.
Inputs may be any that keep to these rules, and one draw needn't show every extreme that they name: `expert_ids`: in each micro-batch, the 8 ids of a token differ, and no expert is named by more than 5 of the 64 tokens of one device; some expert reaches 5. `slot_expert`: each expert lies in exactly one slot.
All inputs are finite; a program needn't handle non-finite values.
Results may differ from the reference program's by a relative error of at most 0.0057.
Values may be sent and summed in bfloat16 or wider, within the bound.
A program may use at most 192 MiB of HBM per device.

```python
import math
import jax
import jax.numpy as jnp
import numpy as np
from jax import lax

D = 3584
FF = 1024
TOPK = 8
MB = 2
TOK_DEV = 64
EXPERTS = 128
TOKENS = 8192
CAP = 5
N_DP = 2
N_EXPERT = 64


def level_of(own_key, dims, cuts, low, high):
    def one(position, shards_of):
        heights = jax.random.uniform(jax.random.fold_in(jax.random.fold_in(own_key, 6), position), (shards_of,), jnp.float32, low / len(cuts), high / len(cuts))
        return jnp.repeat(jnp.exp(heights), dims[position] // shards_of).reshape((-1,) + (1,) * (len(dims) - position - 1))

    level = one(*cuts[0])
    for cut in cuts[1:]:
        level = level * one(*cut)
    return level


def routed_block(own_key, own, number, rows, amount, top, reach, slope):
    ranking = jax.random.permutation(own_key, amount)
    packed, ordinary = shares(amount, rows * top, reach, slope, True), shares(amount, rows * top, reach, slope, False)
    places = jnp.arange(amount)

    def named(lengths, rotation):
        used = int((lengths > 0).sum())
        fixed = max(1, used // 4)
        moved = fixed + (places - fixed + rotation * (used - fixed)) % max(1, amount - fixed)
        return jnp.zeros((amount,), jnp.int32).at[ranking[jnp.where(places < fixed, places, moved)]].set(jnp.asarray(lengths, jnp.int32))

    lengths = jnp.where(number % 4 == 0, named(packed, number // 4), named(ordinary, number - number // 4 - 1))
    mixed = jax.random.permutation(jax.random.fold_in(own, 3), amount)
    source_of, receiver = mixed[0:amount // 2 * 2:2], mixed[1:amount // 2 * 2:2]
    room = jnp.minimum(lengths[source_of] - 1, reach - lengths[receiver]) // 2
    room = jnp.where((source_of == ranking[0]) | (receiver == ranking[0]) | (lengths[receiver] == 0), 0, jnp.maximum(room, 0))
    moved = jax.random.randint(jax.random.fold_in(own, 4), (amount // 2,), 0, 1 << 20) % (room + 1)
    lengths = lengths.at[source_of].add(-moved).at[receiver].add(moved)
    labels = jnp.searchsorted(jnp.cumsum(lengths), jnp.arange(rows * top), side="right").astype(jnp.int32)
    listing = labels.reshape(top, rows).T
    listing = listing[jax.random.permutation(jax.random.fold_in(own, 1), rows)]
    rotation = jax.random.randint(jax.random.fold_in(own, 2), (rows, 1), 0, top)
    return jnp.take_along_axis(listing, (jnp.arange(top)[None, :] + rotation) % top, axis=1)


def shares(number_of, total, most, skew, full):
    portions = [(1 << 20) // math.isqrt(rank ** skew) + 1 for rank in range(1, number_of + 1)]
    largest = most if full else min(most, max(-(-total // number_of), total * portions[0] // sum(portions)))
    least = 1 if total - largest >= number_of - 1 else 0
    given, rest = [largest] + [least] * (number_of - 1), total - largest - least * (number_of - 1)
    while rest > 0:
        free = [i for i in range(1, number_of) if given[i] < largest] or [i for i in range(1, number_of) if given[i] < most]
        mass, left = sum([portions[i] for i in free]), rest
        for i in free:
            addition = min(most - given[i], max(1, left * portions[i] // mass), rest)
            given[i] = given[i] + addition
            rest = rest - addition
    return np.array(given)


def centred(own_key, dims, width, limit, shards=(), kind=jnp.bfloat16):
    entries = width * jax.random.normal(own_key, dims, jnp.float32)
    if shards:
        entries = entries * level_of(own_key, dims, shards, -0.22, 0.18)
    return jnp.clip(entries, -limit, limit).astype(kind)


def setup_inputs(seed: int = 0) -> dict:
    key_list = jax.random.split(jax.random.key(seed), 8)
    tokens = centred(key_list[0], (MB, TOKENS, D), 1.0, 6.0, ((1, 128),))
    expert_ids_keys = jax.random.split(jax.random.fold_in(key_list[1], 1), MB * TOKENS // TOK_DEV)
    expert_ids_turns = jax.random.permutation(jax.random.fold_in(key_list[1], 3), MB * TOKENS // TOK_DEV)
    expert_ids = jax.vmap(lambda own, number: routed_block(jax.random.fold_in(key_list[1], 2), own, number, TOK_DEV, EXPERTS, TOPK, CAP, 2))(expert_ids_keys, expert_ids_turns).reshape((MB, TOKENS, TOPK))
    gate_weights = jnp.clip(0.05 + 0.55 * jax.random.uniform(key_list[2], (MB, TOKENS, TOPK), jnp.float32) ** level_of(key_list[2], (MB, TOKENS, TOPK), ((1, 128),), -0.2, 0.2), 0.05, 0.6)
    slot_expert = jax.random.permutation(key_list[3], EXPERTS).astype(jnp.int32)
    w_gate = centred(key_list[4], (EXPERTS, D, FF), D ** -0.5, 0.09375, ((0, 128),))
    w_up = centred(key_list[5], (EXPERTS, D, FF), D ** -0.5, 0.09375, ((0, 128),))
    w_down = centred(key_list[6], (EXPERTS, FF, D), FF ** -0.5, 0.1875, ((0, 128),))
    return dict(tokens=tokens, expert_ids=expert_ids, gate_weights=gate_weights, slot_expert=slot_expert, w_gate=w_gate, w_up=w_up, w_down=w_down)


def reference(tokens, expert_ids, gate_weights, slot_expert, w_gate, w_up, w_down):
    rows = N_DP * N_EXPERT * CAP
    outputs = []
    for batch in range(MB):
        flat_ids = expert_ids[batch].reshape(-1)
        flat_gates = gate_weights[batch].reshape(-1).astype(jnp.float32)
        batch_tokens = tokens[batch]

        def serve(total, pieces):
            expert, gate_w, up_w, down_w = pieces
            match = flat_ids == expert
            where = jnp.nonzero(match, size=rows, fill_value=0)[0].astype(jnp.int32)
            live = jnp.arange(rows, dtype=jnp.int32) < jnp.sum(match.astype(jnp.int32))
            token_rows = (where // TOPK).astype(jnp.int32)
            chosen = batch_tokens[token_rows]
            gate = jnp.dot(chosen, gate_w, preferred_element_type=jnp.float32)
            up = jnp.dot(chosen, up_w, preferred_element_type=jnp.float32)
            hidden = (jax.nn.silu(gate) * up).astype(jnp.bfloat16)
            result = jnp.dot(hidden, down_w, preferred_element_type=jnp.float32).astype(jnp.bfloat16)
            weight = jnp.where(live, flat_gates[where], jnp.float32(0.0))
            total = total.at[token_rows].add(weight[:, None] * result.astype(jnp.float32))
            return total, None

        start = jnp.zeros((TOKENS, D), jnp.float32)
        total, _ = lax.scan(serve, start, (slot_expert, w_gate, w_up, w_down))
        outputs.append(total.astype(jnp.bfloat16))
    return jnp.stack(outputs, axis=0)
```

```python
import jax
import jax.numpy as jnp
from jax import lax
from jax.experimental import pallas as pl
from jax.experimental.pallas import tpu as pltpu
from jax.sharding import PartitionSpec as P

MESH = pl.DeviceIdType.MESH
BF = jnp.bfloat16
F32 = jnp.float32
I32 = jnp.int32

AXES = ((0, 1, 2), (1, 2, 0), (2, 0, 1))
CAP = 5
RING = (1, 3, 2)
LAST = tuple((dl, dc) for dl in (1, 3, 2, 0) for dc in (0, 1) if (dl, dc) != (0, 0))


def dot(a, b):
    return jnp.dot(a, b, preferred_element_type=F32)


def device_at(pos):
    z, y, x, c = pos
    return (y // 2, ((z * 2 + y % 2) * 4 + x) * 2 + c)


def moved(pos, axis, by, core=0):
    out = list(pos)
    out[axis] = (pos[axis] + by) % 4
    if core:
        out[3] = 1 - pos[3]
    return tuple(out)


def kernel(
    sizes, tokens, ids, gates, slots, w_gate, w_up, w_down, out,
    tok_all, stage, mid, last, fin, info, hidden, hid_f, pick, comb, swap, rot, rot_t,
    wgu, wd, sem_send, sem_recv, sem_local, sem_info_s, sem_info_r, sem_w, sem_wd, free_mid, free_last,
):
    batches, rows_tok, _ = tokens.shape
    starts, widths, tile, tiles = sizes
    dp = lax.axis_index("dp")
    ex = lax.axis_index("expert")
    pos = (ex // 16, dp * 2 + (ex // 8) % 2, (ex // 2) % 4, ex % 2)

    def cols(f):
        return pl.ds(starts[f], widths[f])

    def block(i, n):
        return pl.ds(pl.multiple_of(i * n, n), n)

    peers = [(a, by, c) for a in range(3) for by in (1, 2, 3) for c in (0, 1)] + [(0, 0, 1)]
    barrier = pltpu.get_barrier_semaphore()
    for a, by, c in peers:
        pl.semaphore_signal(barrier, inc=1, device_id=device_at(moved(pos, a, by, c)), device_id_type=MESH)
    pl.semaphore_wait(barrier, len(peers))

    def remote(src, dst, m, f, send, recv, target):
        return pltpu.make_async_remote_copy(
            src_ref=src, dst_ref=dst, send_sem=sem_send.at[m, f, send], recv_sem=sem_recv.at[m, f, recv],
            device_id=device_at(target), device_id_type=MESH,
        )

    def own(src, dst, m, f):
        return pltpu.make_async_copy(src, dst, sem_local.at[m, f])

    def once(make):
        held = {}

        def get(m, f):
            if (m, f) not in held:
                held[m, f] = make(m, f)
            return held[m, f]

        return get

    @once
    def phase1(m, f):
        b = AXES[f][0]
        src = tokens.at[m, :, cols(f)]
        dst = tok_all.at[m, pos[b], :, cols(f)]
        far = [remote(src, dst, m, f, i, i, moved(pos, b, by)) for i, by in enumerate(RING)]
        return far, own(src, dst, m, f)

    def along_mid(m, f, base):
        a = AXES[f][1]

        def src(to):
            return stage.at[m, block(to, 160), cols(f)]

        dst = mid.at[m, block(pos[a], 160), cols(f)]
        far = [
            remote(src((pos[a] + by) % 4), dst, m, f, i, base + i, moved(pos, a, by)) for i, by in enumerate(RING)
        ]
        return far, own(src(pos[a]), dst, m, f)

    def along_last(m, f, base):
        a = AXES[f][2]

        def src(to, core):
            return stage.at[m, block(core * 4 + to, 80), cols(f)]

        dst = last.at[m, block(pos[3] * 4 + pos[a], 80), cols(f)]
        far = [
            remote(
                src((pos[a] + by) % 4, 1 - pos[3] if dc else pos[3]), dst, m, f, i, base + i, moved(pos, a, by, dc)
            )
            for i, (by, dc) in enumerate(LAST)
        ]
        return far, own(src(pos[a], pos[3]), dst, m, f)

    @once
    def phase2(m, f):
        return along_mid(m, f, 3)

    @once
    def phase3(m, f):
        return along_last(m, f, 6)

    @once
    def back3(m, f):
        return along_last(m, f, 13)

    @once
    def back2(m, f):
        return along_mid(m, f, 20)

    @once
    def back1(m, f):
        b = AXES[f][0]
        far = [
            remote(
                tok_all.at[m, (pos[b] + by) % 4, :, cols(f)], fin.at[m, i, :, cols(f)], m, f, i, 23 + i,
                moved(pos, b, by),
            )
            for i, by in enumerate(RING)
        ]
        return far, None

    def start(copies):
        far, near = copies
        for copy in far:
            copy.start()
        if near is not None:
            near.start()

    def arrive(copies):
        far, near = copies
        for copy in far:
            copy.wait_recv()
        if near is not None:
            near.wait()

    def sent(copies):
        for copy in copies[0]:
            copy.wait_send()

    def load_tile(j, slot):
        at = pl.ds(pl.multiple_of(j * tile, tile), tile)
        return (
            pltpu.make_async_copy(w_gate.at[0, :, at], wgu.at[slot, 0], sem_w.at[slot, 0]),
            pltpu.make_async_copy(w_up.at[0, :, at], wgu.at[slot, 1], sem_w.at[slot, 1]),
        )

    for m in range(batches):
        for f in range(3):
            start(phase1(m, f))
    load_down = pltpu.make_async_copy(w_down.at[0], wd, sem_wd)
    load_down.start()
    for slot in range(2):
        for copy in load_tile(slot, slot):
            copy.start()

    sub = lax.broadcasted_iota(I32, (128, 128), 0)
    lane = lax.broadcasted_iota(I32, (128, 128), 1)
    holder = jnp.sum(jnp.where(slots[...] == sub, lane, 0).astype(F32), axis=1, keepdims=True) * 8.0
    before = jnp.where((sub < 64) & (sub < lane % 64), 1.0, 0.0).astype(BF)
    lane8 = lax.broadcasted_iota(I32, (8, 128), 1)
    for m in range(batches):
        names = ids[m]
        same = [names[k : k + 1, :] == sub for k in range(8)]
        chosen = jnp.where(same[0], 1.0, 0.0)
        for k in range(1, 8):
            chosen = chosen + jnp.where(same[k], 1.0, 0.0)
        value = dot(chosen.astype(BF), before) + holder
        found = jnp.concatenate(
            [jnp.sum(jnp.where(same[k], value, 0.0), axis=0, keepdims=True) for k in range(8)], axis=0
        ).astype(I32)
        rank = found & 7
        where = found >> 3
        at = (
            (where >> 4) & 3,
            ((where >> 3) & 1) + ((where >> 6) & 1) * 2,
            (where >> 1) & 3,
            where & 1,
        )
        for f in range(3):
            b, a, l = AXES[f]
            key = at[b] * 640 + at[a] * 160 + (at[3] * 4 + at[l]) * 20 + pos[b] * CAP + rank
            mine = (lane8 >= 64) == (lax.broadcast(pos[b] % 2, (8, 128)) == 1)
            info[f, pos[b], m, 0:8, :] = jnp.where(mine, key.astype(F32), -1.0)
            info[f, pos[b], m, 8:16, :] = jnp.where(mine, gates[m], 0.0)
    tell = []
    for f in range(3):
        b = AXES[f][0]
        for i, by in enumerate(RING):
            tell.append(
                pltpu.make_async_remote_copy(
                    src_ref=info.at[f, pos[b]], dst_ref=info.at[f, pos[b]], send_sem=sem_info_s.at[f, i],
                    recv_sem=sem_info_r.at[f, i], device_id=device_at(moved(pos, b, by)), device_id_type=MESH,
                )
            )
    for copy in tell:
        copy.start()

    r = lax.broadcasted_iota(I32, (320, 320), 0)
    n = lax.broadcasted_iota(I32, (320, 320), 1)
    fifth = (r * 205) >> 10
    d0, d1, d2, d3 = fifth >> 4, (fifth >> 2) & 3, fifth & 3, r - fifth * 5
    swap[...] = jnp.where(n == d1 * 80 + d0 * 20 + d2 * 5 + d3, 1.0, 0.0).astype(BF)
    rot[...] = jnp.where(n == d2 * 80 + d0 * 20 + d1 * 5 + d3, 1.0, 0.0).astype(BF)
    rot_t[...] = jnp.where(n == d1 * 80 + d2 * 20 + d0 * 5 + d3, 1.0, 0.0).astype(BF)

    for copy in tell:
        copy.wait()

    def keys(m, f):
        low = jnp.maximum(info[f, 0, m, 0:8, :], info[f, 1, m, 0:8, :])
        high = jnp.maximum(info[f, 2, m, 0:8, :], info[f, 3, m, 0:8, :])
        return jnp.concatenate([low, high], axis=1)

    def weights(m, f):
        low = info[f, 0, m, 8:16, :] + info[f, 1, m, 8:16, :]
        high = info[f, 2, m, 8:16, :] + info[f, 3, m, 8:16, :]
        return jnp.concatenate([low, high], axis=1)

    def row_key(f, i):
        return (lax.broadcasted_iota(I32, (128, 256), 0) + (pos[AXES[f][0]] * 640 + i * 128)).astype(F32)

    def build_pick(m, f):
        key = keys(m, f)
        for i in range(5):
            row = row_key(f, i)
            hit = key[0:1, :] == row
            for k in range(1, 8):
                hit = hit | (key[k : k + 1, :] == row)
            pick[i * 128 : (i + 1) * 128, :] = jnp.where(hit, 1.0, 0.0).astype(BF)

    def build_comb(m, f):
        key = keys(m, f)
        gate = weights(m, f)
        for i in range(5):
            row = row_key(f, i)
            total = jnp.zeros((128, 256), F32)
            for k in range(8):
                total = jnp.where(key[k : k + 1, :] == row, gate[k : k + 1, :], total)
            comb[m, f, :, i * 128 : (i + 1) * 128] = total.T.astype(BF)

    def chunks(f):
        at = 0
        while at < widths[f]:
            size = min(512, widths[f] - at)
            yield starts[f] + at, size
            at += size

    def step1(m, f):
        build_pick(m, f)
        arrive(phase1(m, f))
        for at, size in chunks(f):
            rows = tok_all[m, :, :, at : at + size].reshape(4 * rows_tok, size)
            stage[m, :, at : at + size] = dot(pick[...], rows).astype(BF)
        sent(phase1(m, f))
        start(phase2(m, f))

    def step2(m, f):
        arrive(phase2(m, f))
        sent(phase2(m, f))
        for at, size in chunks(f):
            for c in range(2):
                rows = jnp.concatenate(
                    [mid[m, i * 160 + c * 80 : i * 160 + c * 80 + 80, at : at + size] for i in range(4)], axis=0
                )
                stage[m, c * 320 : c * 320 + 320, at : at + size] = dot(swap[...], rows).astype(BF)
        for by in RING:
            pl.semaphore_signal(
                free_mid.at[m, f], inc=1, device_id=device_at(moved(pos, AXES[f][1], by)), device_id_type=MESH
            )
        start(phase3(m, f))

    def gather(m, f):
        arrive(phase3(m, f))
        sent(phase3(m, f))
        for at, size in chunks(f):
            for c in range(2):
                rows = last[m, c * 320 : c * 320 + 320, at : at + size]
                if f:
                    rows = dot((rot, rot_t)[f - 1][...], rows).astype(BF)
                stage[m, c * 320 : c * 320 + 320, at : at + size] = rows
        for by, dc in LAST:
            pl.semaphore_signal(
                free_last.at[m, f], inc=1, device_id=device_at(moved(pos, AXES[f][2], by, dc)), device_id_type=MESH
            )

    def expand(m):
        def one(j, carry):
            slot = j % 2
            for copy in load_tile(j, slot):
                copy.wait()

            def half(i, carry):
                at = pl.ds(pl.multiple_of(i * 320, 320), 320)
                rows = stage[m, at, :]
                gate = dot(rows, wgu[slot, 0])
                up = dot(rows, wgu[slot, 1])
                hidden[at, pl.ds(pl.multiple_of(j * tile, tile), tile)] = (gate / (1.0 + jnp.exp(-gate)) * up).astype(BF)
                return carry

            lax.fori_loop(0, 2, half, 0)
            following = j + 2 if m + 1 == batches else (j + 2) % tiles

            def more():
                for copy in load_tile(following, slot):
                    copy.start()

            if m + 1 == batches:
                pl.when(following < tiles)(more)
            else:
                more()
            return carry

        lax.fori_loop(0, tiles, one, 0)

    def shrink(m, f):
        if f:
            for c in range(2):
                hid_f[c * 320 : c * 320 + 320, :] = dot(
                    (rot_t, rot)[f - 1][...], hidden[c * 320 : c * 320 + 320, :]
                ).astype(BF)
        rows = (hid_f if f else hidden)[...]
        for at, size in chunks(f):
            stage[m, :, at : at + size] = dot(rows, wd[:, at : at + size]).astype(BF)
        pl.semaphore_wait(free_last.at[m, f], len(LAST))
        start(back3(m, f))

    def step4(m, f):
        arrive(back3(m, f))
        sent(back3(m, f))
        for at, size in chunks(f):
            for c in range(2):
                rows = dot(swap[...], last[m, c * 320 : c * 320 + 320, at : at + size]).astype(BF)
                for i in range(4):
                    stage[m, i * 160 + c * 80 : i * 160 + c * 80 + 80, at : at + size] = rows[i * 80 : i * 80 + 80, :]
        pl.semaphore_wait(free_mid.at[m, f], len(RING))
        start(back2(m, f))

    def step5(m, f):
        arrive(back2(m, f))
        sent(back2(m, f))
        for at, size in chunks(f):
            rows = dot(comb[m, f], mid[m, :, at : at + size]).astype(BF)
            tok_all[m, :, :, at : at + size] = rows.reshape(4, rows_tok, size)
        start(back1(m, f))

    def step6(m, f):
        arrive(back1(m, f))
        total = tok_all[m, pos[AXES[f][0]], :, cols(f)].astype(F32)
        for i in range(3):
            total = total + fin[m, i, :, cols(f)].astype(F32)
        out[m, :, cols(f)] = total.astype(BF)
        sent(back1(m, f))

    parts = range(3)
    for m in range(batches):
        for f in parts:
            step1(m, f)
    for m in range(batches):
        for f in parts:
            build_comb(m, f)
    for m in range(batches):
        for f in parts:
            step2(m, f)
    load_down.wait()
    for m in range(batches):
        for f in parts:
            gather(m, f)
        expand(m)
        for f in parts:
            shrink(m, f)
    for m in range(batches):
        for f in parts:
            step4(m, f)
    for m in range(batches):
        for f in parts:
            step5(m, f)
    for m in range(batches):
        for f in parts:
            step6(m, f)


def local(tokens, expert_ids, gate_weights, slot_expert, w_gate, w_up, w_down):
    batches, rows, width = tokens.shape
    ff = w_gate.shape[2]
    slots = 128 * CAP
    unit = width // 128
    widths = (unit // 3 * 128, unit // 3 * 128, (unit - 2 * (unit // 3)) * 128)
    starts = (0, widths[0], widths[0] + widths[1])
    tile = 256
    tiles = ff // tile

    def lanes(a):
        turned = jnp.swapaxes(a, 1, 2)
        return jnp.concatenate([turned, turned], axis=2)

    vmem = pl.BlockSpec(memory_space=pltpu.VMEM)
    hbm = pl.BlockSpec(memory_space=pl.ANY)

    def body(*refs):
        kernel((starts, widths, tile, tiles), *refs)

    return pl.pallas_call(
        body,
        out_shape=jax.ShapeDtypeStruct(tokens.shape, BF),
        in_specs=[hbm, vmem, vmem, vmem, hbm, hbm, hbm],
        out_specs=vmem,
        scratch_shapes=[
            pltpu.VMEM((batches, 4, rows, width), BF),
            pltpu.VMEM((batches, slots, width), BF),
            pltpu.VMEM((batches, slots, width), BF),
            pltpu.VMEM((batches, slots, width), BF),
            pltpu.VMEM((batches, 3, rows, width), BF),
            pltpu.VMEM((3, 4, batches, 16, 128), F32),
            pltpu.VMEM((slots, ff), BF),
            pltpu.VMEM((slots, ff), BF),
            pltpu.VMEM((slots, 4 * rows), BF),
            pltpu.VMEM((batches, 3, 4 * rows, slots), BF),
            pltpu.VMEM((320, 320), BF),
            pltpu.VMEM((320, 320), BF),
            pltpu.VMEM((320, 320), BF),
            pltpu.VMEM((2, 2, width, tile), BF),
            pltpu.VMEM((ff, width), BF),
            pltpu.SemaphoreType.DMA((batches, 3, 7)),
            pltpu.SemaphoreType.DMA((batches, 3, 26)),
            pltpu.SemaphoreType.DMA((batches, 3)),
            pltpu.SemaphoreType.DMA((3, 3)),
            pltpu.SemaphoreType.DMA((3, 3)),
            pltpu.SemaphoreType.DMA((2, 2)),
            pltpu.SemaphoreType.DMA,
            pltpu.SemaphoreType.REGULAR((batches, 3)),
            pltpu.SemaphoreType.REGULAR((batches, 3)),
        ],
        compiler_params=pltpu.CompilerParams(collective_id=0, has_side_effects=True, vmem_limit_bytes=62 << 20),
        cost_estimate=pl.CostEstimate(flops=60 * 10**9, bytes_accessed=24 * 10**6, transcendentals=10**6),
    )(tokens, lanes(expert_ids), lanes(gate_weights), slot_expert.reshape(1, -1), w_gate, w_up, w_down)


def solution(mesh):
    in_specs = (
        P(None, ("dp", "expert"), None),
        P(None, ("dp", "expert"), None),
        P(None, ("dp", "expert"), None),
        P(),
        P(("dp", "expert"), None, None),
        P(("dp", "expert"), None, None),
        P(("dp", "expert"), None, None),
    )
    out_specs = P(None, ("dp", "expert"), None)
    return jax.shard_map(local, mesh=mesh, in_specs=in_specs, out_specs=out_specs, check_vma=False)
```

```python
import jax
import jax.numpy as jnp
from jax import lax
from jax.experimental import pallas as pl
from jax.experimental.pallas import tpu as pltpu
from jax.sharding import PartitionSpec as P

MESH = pl.DeviceIdType.MESH
BF = jnp.bfloat16
F32 = jnp.float32
I32 = jnp.int32

AXES = ((0, 1, 2), (1, 2, 0), (2, 0, 1))
CAP = 5
RING = (1, 3, 2)
LAST = tuple((dl, dc) for dl in (1, 3, 2, 0) for dc in (0, 1) if (dl, dc) != (0, 0))


def dot(a, b):
    return jnp.dot(a, b, preferred_element_type=F32)


def device_at(pos):
    z, y, x, c = pos
    return (y // 2, ((z * 2 + y % 2) * 4 + x) * 2 + c)


def moved(pos, axis, by, core=0):
    out = list(pos)
    out[axis] = (pos[axis] + by) % 4
    if core:
        out[3] = 1 - pos[3]
    return tuple(out)


def kernel(
    sizes, tokens, ids, gates, slots, w_gate, w_up, w_down, out,
    tok_all, stage, mid, last, fin, info, hidden, pick, comb, swap, rot, rot_t,
    wg, wu, wd, sem_send, sem_recv, sem_local, sem_info_s, sem_info_r, sem_w, free_mid, free_last,
):
    batches, rows_tok, _ = tokens.shape
    starts, widths, tile, tiles = sizes
    dp = lax.axis_index("dp")
    ex = lax.axis_index("expert")
    pos = (ex // 16, dp * 2 + (ex // 8) % 2, (ex // 2) % 4, ex % 2)

    def cols(f):
        return pl.ds(starts[f], widths[f])

    def block(i, n):
        return pl.ds(pl.multiple_of(i * n, n), n)

    peers = [(a, by, c) for a in range(3) for by in (1, 2, 3) for c in (0, 1)] + [(0, 0, 1)]
    barrier = pltpu.get_barrier_semaphore()
    for a, by, c in peers:
        pl.semaphore_signal(barrier, inc=1, device_id=device_at(moved(pos, a, by, c)), device_id_type=MESH)
    sub = lax.broadcasted_iota(I32, (128, 128), 0)
    lane = lax.broadcasted_iota(I32, (128, 128), 1)
    holder = jnp.sum(jnp.where(slots[...] == sub, lane, 0).astype(F32), axis=1, keepdims=True) * 8.0
    before = jnp.where((sub < 64) & (sub < lane % 64), 1.0, 0.0).astype(BF)
    lane8 = lax.broadcasted_iota(I32, (8, 128), 1)
    twice = jnp.where(sub[:64] == lane[:64] % 64, 1.0, 0.0).astype(BF)

    def turned(rows):
        return lax.dot_general(rows.astype(BF), twice, (((0,), (0,)), ((), ())), preferred_element_type=F32)

    for m in range(batches):
        names = turned(ids[m].astype(F32)).astype(I32)
        gate_rows = turned(gates[m])
        same = [names[k : k + 1, :] == sub for k in range(8)]
        chosen = jnp.where(same[0], 1.0, 0.0)
        for k in range(1, 8):
            chosen = chosen + jnp.where(same[k], 1.0, 0.0)
        value = dot(chosen.astype(BF), before) + holder
        found = jnp.concatenate(
            [jnp.sum(jnp.where(same[k], value, 0.0), axis=0, keepdims=True) for k in range(8)], axis=0
        ).astype(I32)
        rank = found & 7
        where = found >> 3
        at = (
            (where >> 4) & 3,
            ((where >> 3) & 1) + ((where >> 6) & 1) * 2,
            (where >> 1) & 3,
            where & 1,
        )
        for f in range(3):
            b, a, l = AXES[f]
            key = at[b] * 640 + at[a] * 160 + (at[3] * 4 + at[l]) * 20 + pos[b] * CAP + rank
            mine = (lane8 >= 64) == (lax.broadcast(pos[b] % 2, (8, 128)) == 1)
            info[f, pos[b], m, 0:8, :] = jnp.where(mine, key.astype(F32), -1.0)
            info[f, pos[b], m, 8:16, :] = jnp.where(mine, gate_rows, 0.0)
    pl.semaphore_wait(barrier, len(peers))

    def remote(src, dst, m, f, send, recv, target):
        return pltpu.make_async_remote_copy(
            src_ref=src, dst_ref=dst, send_sem=sem_send.at[m, f, send], recv_sem=sem_recv.at[m, f, recv],
            device_id=device_at(target), device_id_type=MESH,
        )

    def own(src, dst, m, f):
        return pltpu.make_async_copy(src, dst, sem_local.at[m, f])

    def once(make):
        held = {}

        def get(m, f):
            if (m, f) not in held:
                held[m, f] = make(m, f)
            return held[m, f]

        return get

    @once
    def phase1(m, f):
        b = AXES[f][0]
        src = tokens.at[m, :, cols(f)]
        dst = tok_all.at[m, pos[b], :, cols(f)]
        far = [remote(src, dst, m, f, i, i, moved(pos, b, by)) for i, by in enumerate(RING)]
        return far, own(src, dst, m, f)

    def along_mid(m, f, base):
        a = AXES[f][1]

        def src(to):
            return stage.at[m, block(to, 160), cols(f)]

        dst = mid.at[m, block(pos[a], 160), cols(f)]
        far = [
            remote(src((pos[a] + by) % 4), dst, m, f, i, base + i, moved(pos, a, by)) for i, by in enumerate(RING)
        ]
        return far, own(src(pos[a]), dst, m, f)

    def along_last(m, f, base):
        a = AXES[f][2]

        def src(to, core):
            return stage.at[m, block(core * 4 + to, 80), cols(f)]

        dst = last.at[m, block(pos[3] * 4 + pos[a], 80), cols(f)]
        far = [
            remote(
                src((pos[a] + by) % 4, 1 - pos[3] if dc else pos[3]), dst, m, f, i, base + i, moved(pos, a, by, dc)
            )
            for i, (by, dc) in enumerate(LAST)
        ]
        return far, own(src(pos[a], pos[3]), dst, m, f)

    @once
    def phase2(m, f):
        return along_mid(m, f, 3)

    @once
    def phase3(m, f):
        return along_last(m, f, 6)

    @once
    def back3(m, f):
        return along_last(m, f, 13)

    @once
    def back2(m, f):
        return along_mid(m, f, 20)

    @once
    def back1(m, f):
        b = AXES[f][0]
        far = [
            remote(
                tok_all.at[m, (pos[b] + by) % 4, :, cols(f)], fin.at[m, i, :, cols(f)], m, f, i, 23 + i,
                moved(pos, b, by),
            )
            for i, by in enumerate(RING)
        ]
        return far, None

    def start(copies):
        far, near = copies
        for copy in far:
            copy.start()
        if near is not None:
            near.start()

    def arrive(copies):
        far, near = copies
        for copy in far:
            copy.wait_recv()
        if near is not None:
            near.wait()

    def sent(copies):
        for copy in copies[0]:
            copy.wait_send()

    tell = []
    for f in range(3):
        b = AXES[f][0]
        for i, by in enumerate(RING):
            tell.append(
                pltpu.make_async_remote_copy(
                    src_ref=info.at[f, pos[b]], dst_ref=info.at[f, pos[b]], send_sem=sem_info_s.at[f, i],
                    recv_sem=sem_info_r.at[f, i], device_id=device_at(moved(pos, b, by)), device_id_type=MESH,
                )
            )
    for copy in tell:
        copy.start()

    for m in range(batches):
        for f in range(3):
            start(phase1(m, f))
    loads = [
        pltpu.make_async_copy(src.at[0], dst, sem_w.at[i])
        for i, (src, dst) in enumerate(((w_gate, wg), (w_up, wu), (w_down, wd)))
    ]
    for copy in loads:
        copy.start()

    r = lax.broadcasted_iota(I32, (320, 320), 0)
    n = lax.broadcasted_iota(I32, (320, 320), 1)
    fifth = (r * 205) >> 10
    d0, d1, d2, d3 = fifth >> 4, (fifth >> 2) & 3, fifth & 3, r - fifth * 5
    swap[...] = jnp.where(n == d1 * 80 + d0 * 20 + d2 * 5 + d3, 1.0, 0.0).astype(BF)
    rot[...] = jnp.where(n == d2 * 80 + d0 * 20 + d1 * 5 + d3, 1.0, 0.0).astype(BF)
    rot_t[...] = jnp.where(n == d1 * 80 + d2 * 20 + d0 * 5 + d3, 1.0, 0.0).astype(BF)

    for copy in tell:
        copy.wait()

    def keys(m, f):
        low = jnp.maximum(info[f, 0, m, 0:8, :], info[f, 1, m, 0:8, :])
        high = jnp.maximum(info[f, 2, m, 0:8, :], info[f, 3, m, 0:8, :])
        return jnp.concatenate([low, high], axis=1)

    def weights(m, f):
        low = info[f, 0, m, 8:16, :] + info[f, 1, m, 8:16, :]
        high = info[f, 2, m, 8:16, :] + info[f, 3, m, 8:16, :]
        return jnp.concatenate([low, high], axis=1)

    def row_key(f, i):
        return (lax.broadcasted_iota(I32, (128, 256), 0) + (pos[AXES[f][0]] * 640 + i * 128)).astype(F32)

    def build_pick(m, f):
        key = keys(m, f)
        for i in range(5):
            row = row_key(f, i)
            hit = key[0:1, :] == row
            for k in range(1, 8):
                hit = hit | (key[k : k + 1, :] == row)
            pick[i * 128 : (i + 1) * 128, :] = jnp.where(hit, 1.0, 0.0).astype(BF)

    def build_comb(m, f):
        key = keys(m, f)
        gate = weights(m, f)
        for i in range(5):
            row = row_key(f, i)
            total = jnp.zeros((128, 256), F32)
            for k in range(8):
                total = jnp.where(key[k : k + 1, :] == row, gate[k : k + 1, :], total)
            comb[m, f, :, i * 128 : (i + 1) * 128] = total.T.astype(BF)

    def halves(work):
        def one(c, carry):
            work(c)
            return carry

        lax.fori_loop(0, 2, one, 0)

    def chunks(f):
        at = 0
        while at < widths[f]:
            size = min(512, widths[f] - at)
            yield starts[f] + at, size
            at += size

    def step1(m, f):
        build_pick(m, f)
        phase1(m, f)[1].wait()
        arrive((phase1(m, f)[0], None))
        for at, size in chunks(f):
            rows = tok_all[m, :, :, at : at + size].reshape(4 * rows_tok, size)
            stage[m, :, at : at + size] = dot(pick[...], rows).astype(BF)
        sent(phase1(m, f))
        start(phase2(m, f))

    def step2(m, f):
        arrive(phase2(m, f))
        sent(phase2(m, f))
        @halves
        def _(c):
            for at, size in chunks(f):
                rows = jnp.concatenate(
                    [mid[m, block(i * 2 + c, 80), at : at + size] for i in range(4)], axis=0
                )
                stage[m, block(c, 320), at : at + size] = dot(swap[...], rows).astype(BF)

        for by in RING:
            pl.semaphore_signal(
                free_mid.at[m, f], inc=1, device_id=device_at(moved(pos, AXES[f][1], by)), device_id_type=MESH
            )
        start(phase3(m, f))

    def side(copies, h):
        return [copy for copy, (by, dc) in zip(copies[0], LAST) if dc == h], None if h else copies[1]

    def half(h):
        return block(1 - pos[3] if h else pos[3], 320)

    def gather(m, f, h):
        arrive(side(phase3(m, f), h))
        if h == 0:
            sent(phase3(m, f))
        for at, size in chunks(f):
            rows = last[m, half(h), at : at + size]
            if f:
                rows = dot((rot, rot_t)[f - 1][...], rows).astype(BF)
            stage[m, half(h), at : at + size] = rows
        for by, dc in LAST:
            if dc == h:
                pl.semaphore_signal(
                    free_last.at[m, f, h], inc=1, device_id=device_at(moved(pos, AXES[f][2], by, dc)),
                    device_id_type=MESH,
                )

    def expand(m, h):
        def one(j, carry):
            at = pl.ds(pl.multiple_of(j * tile, tile), tile)
            rows = stage[m, half(h), :]
            gate = dot(rows, wg[:, at])
            up = dot(rows, wu[:, at])
            hidden[:, at] = (gate / (1.0 + jnp.exp(-gate)) * up).astype(BF)
            return carry

        lax.fori_loop(0, tiles, one, 0)

    def shrink(m, f, h):
        rows = hidden[...]
        if f:
            rows = dot((rot_t, rot)[f - 1][...], rows).astype(BF)
        for at, size in chunks(f):
            stage[m, half(h), at : at + size] = dot(rows, wd[:, at : at + size]).astype(BF)
        pl.semaphore_wait(free_last.at[m, f, h], 3 + h)
        start(side(back3(m, f), h))

    def step4(m, f):
        arrive(back3(m, f))
        sent(back3(m, f))
        @halves
        def _(c):
            for at, size in chunks(f):
                rows = dot(swap[...], last[m, block(c, 320), at : at + size]).astype(BF)
                for i in range(4):
                    stage[m, block(i * 2 + c, 80), at : at + size] = rows[i * 80 : i * 80 + 80, :]

        pl.semaphore_wait(free_mid.at[m, f], len(RING))
        start(back2(m, f))

    def step5(m, f):
        arrive(back2(m, f))
        sent(back2(m, f))
        for at, size in chunks(f):
            rows = dot(comb[m, f], mid[m, :, at : at + size]).astype(BF)
            tok_all[m, :, :, at : at + size] = rows.reshape(4, rows_tok, size)
        start(back1(m, f))

    @once
    def leave(m, f):
        return own(tok_all.at[m, pos[AXES[f][0]], :, cols(f)], out.at[m, :, cols(f)], m, f)

    def step6(m, f):
        arrive(back1(m, f))
        total = tok_all[m, pos[AXES[f][0]], :, cols(f)].astype(F32)
        for i in range(3):
            total = total + fin[m, i, :, cols(f)].astype(F32)
        tok_all[m, pos[AXES[f][0]], :, cols(f)] = total.astype(BF)
        leave(m, f).start()
        sent(back1(m, f))

    parts = range(3)
    for f in parts:
        step1(0, f)
    for f in parts:
        step1(1, f)
    for f in parts:
        build_comb(0, f)
    for f in parts:
        build_comb(1, f)
    for f in parts:
        step2(0, f)
    for f in parts:
        step2(1, f)
    for copy in loads:
        copy.wait()
    for f in parts:
        gather(0, f, 0)
    expand(0, 0)
    for f in parts:
        shrink(0, f, 0)
    for f in parts:
        gather(0, f, 1)
    expand(0, 1)
    for f in parts:
        shrink(0, f, 1)
    for f in parts:
        gather(1, f, 0)
    expand(1, 0)
    for f in parts:
        shrink(1, f, 0)
    for f in parts:
        gather(1, f, 1)
    expand(1, 1)
    for f in parts:
        shrink(1, f, 1)
    for f in parts:
        step4(0, f)
    for f in parts:
        step4(1, f)
    for f in parts:
        step5(0, f)
    for f in parts:
        step5(1, f)
    for f in parts:
        step6(0, f)
    for f in parts:
        step6(1, f)
    for f in parts:
        leave(0, f).wait()
    for f in parts:
        leave(1, f).wait()


def local(tokens, expert_ids, gate_weights, slot_expert, w_gate, w_up, w_down):
    batches, rows, width = tokens.shape
    ff = w_gate.shape[2]
    slots = 128 * CAP
    unit = width // 128
    widths = (unit // 3 * 128, unit // 3 * 128, (unit - 2 * (unit // 3)) * 128)
    starts = (0, widths[0], widths[0] + widths[1])
    tile = 256
    tiles = ff // tile

    vmem = pl.BlockSpec(memory_space=pltpu.VMEM)
    hbm = pl.BlockSpec(memory_space=pl.ANY)

    def body(*refs):
        kernel((starts, widths, tile, tiles), *refs)

    return pl.pallas_call(
        body,
        out_shape=jax.ShapeDtypeStruct(tokens.shape, BF),
        in_specs=[hbm, vmem, vmem, vmem, hbm, hbm, hbm],
        out_specs=hbm,
        scratch_shapes=[
            pltpu.VMEM((batches, 4, rows, width), BF),
            pltpu.VMEM((batches, slots, width), BF),
            pltpu.VMEM((batches, slots, width), BF),
            pltpu.VMEM((batches, slots, width), BF),
            pltpu.VMEM((batches, 3, rows, width), BF),
            pltpu.VMEM((3, 4, batches, 16, 128), F32),
            pltpu.VMEM((slots // 2, ff), BF),
            pltpu.VMEM((slots, 4 * rows), BF),
            pltpu.VMEM((batches, 3, 4 * rows, slots), BF),
            pltpu.VMEM((320, 320), BF),
            pltpu.VMEM((320, 320), BF),
            pltpu.VMEM((320, 320), BF),
            pltpu.VMEM((width, ff), BF),
            pltpu.VMEM((width, ff), BF),
            pltpu.VMEM((ff, width), BF),
            pltpu.SemaphoreType.DMA((batches, 3, 7)),
            pltpu.SemaphoreType.DMA((batches, 3, 26)),
            pltpu.SemaphoreType.DMA((batches, 3)),
            pltpu.SemaphoreType.DMA((3, 3)),
            pltpu.SemaphoreType.DMA((3, 3)),
            pltpu.SemaphoreType.DMA((3,)),
            pltpu.SemaphoreType.REGULAR((batches, 3)),
            pltpu.SemaphoreType.REGULAR((batches, 3, 2)),
        ],
        compiler_params=pltpu.CompilerParams(collective_id=0, has_side_effects=True, vmem_limit_bytes=62 << 20),
        cost_estimate=pl.CostEstimate(flops=60 * 10**9, bytes_accessed=24 * 10**6, transcendentals=10**6),
    )(tokens, expert_ids, gate_weights, slot_expert.reshape(1, -1), w_gate, w_up, w_down)


def solution(mesh):
    in_specs = (
        P(None, ("dp", "expert"), None),
        P(None, ("dp", "expert"), None),
        P(None, ("dp", "expert"), None),
        P(),
        P(("dp", "expert"), None, None),
        P(("dp", "expert"), None, None),
        P(("dp", "expert"), None, None),
    )
    out_specs = P(None, ("dp", "expert"), None)
    return jax.shard_map(local, mesh=mesh, in_specs=in_specs, out_specs=out_specs, check_vma=False)
```

```python
import jax
import jax.numpy as jnp
from jax import lax
from jax.experimental import pallas as pl
from jax.experimental.pallas import tpu as pltpu
from jax.sharding import PartitionSpec as P

MESH = pl.DeviceIdType.MESH
BF = jnp.bfloat16
F32 = jnp.float32
I32 = jnp.int32

AXES = ((0, 1, 2), (1, 2, 0), (2, 0, 1))
CAP = 5
RING = (1, 3, 2)
LAST = tuple((dl, dc) for dl in (1, 3, 2, 0) for dc in (0, 1) if (dl, dc) != (0, 0))


def dot(a, b):
    return jnp.dot(a, b, preferred_element_type=F32)


def device_at(pos):
    z, y, x, c = pos
    return (y // 2, ((z * 2 + y % 2) * 4 + x) * 2 + c)


def moved(pos, axis, by, core=0):
    out = list(pos)
    out[axis] = (pos[axis] + by) % 4
    if core:
        out[3] = 1 - pos[3]
    return tuple(out)


def kernel(
    sizes, tokens, ids, gates, slots, w_gate, w_up, w_down, out,
    tok_all, stage, mid, last, fin, info, hidden, pick, comb, swap, rot, rot_t,
    wg, wu, wd, sem_send, sem_recv, sem_local, sem_info_s, sem_info_r, sem_w, free_mid, free_last,
):
    batches, rows_tok, _ = tokens.shape
    starts, widths, tile, tiles = sizes
    dp = lax.axis_index("dp")
    ex = lax.axis_index("expert")
    pos = (ex // 16, dp * 2 + (ex // 8) % 2, (ex // 2) % 4, ex % 2)

    def cols(m, f):
        return pl.ds(starts[m][f], widths[m][f])

    def block(i, n):
        return pl.ds(pl.multiple_of(i * n, n), n)

    peers = [(a, by, c) for a in range(3) for by in (1, 2, 3) for c in (0, 1)] + [(0, 0, 1)]
    barrier = pltpu.get_barrier_semaphore()
    for a, by, c in peers:
        pl.semaphore_signal(barrier, inc=1, device_id=device_at(moved(pos, a, by, c)), device_id_type=MESH)
    sub = lax.broadcasted_iota(I32, (128, 128), 0)
    lane = lax.broadcasted_iota(I32, (128, 128), 1)
    holder = jnp.sum(jnp.where(slots[...] == sub, lane, 0).astype(F32), axis=1, keepdims=True) * 8.0
    before = jnp.where((sub < 64) & (sub < lane % 64), 1.0, 0.0).astype(BF)
    lane8 = lax.broadcasted_iota(I32, (8, 128), 1)
    twice = jnp.where(sub[:64] == lane[:64] % 64, 1.0, 0.0).astype(BF)

    for m in range(batches):
        names = dot(ids[m].astype(F32).astype(BF), twice).astype(I32)
        gate_rows = dot(gates[m].astype(BF), twice)
        same = [names[k : k + 1, :] == sub for k in range(8)]
        chosen = jnp.where(same[0], 1.0, 0.0)
        for k in range(1, 8):
            chosen = chosen + jnp.where(same[k], 1.0, 0.0)
        value = dot(chosen.astype(BF), before) + holder
        found = jnp.concatenate(
            [jnp.sum(jnp.where(same[k], value, 0.0), axis=0, keepdims=True) for k in range(8)], axis=0
        ).astype(I32)
        rank = found & 7
        where = found >> 3
        at = (
            (where >> 4) & 3,
            ((where >> 3) & 1) + ((where >> 6) & 1) * 2,
            (where >> 1) & 3,
            where & 1,
        )
        for f in range(3):
            b, a, l = AXES[f]
            key = at[b] * 640 + at[a] * 160 + (at[3] * 4 + at[l]) * 20 + pos[b] * CAP + rank
            mine = (lane8 >= 64) == (lax.broadcast(pos[b] % 2, (8, 128)) == 1)
            info[f, pos[b], m, 0:8, :] = jnp.where(mine, key.astype(F32), -1.0)
            info[f, pos[b], m, 8:16, :] = jnp.where(mine, gate_rows, 0.0)
    pl.semaphore_wait(barrier, len(peers))

    def remote(src, dst, m, f, send, recv, target):
        return pltpu.make_async_remote_copy(
            src_ref=src, dst_ref=dst, send_sem=sem_send.at[m, f, send], recv_sem=sem_recv.at[m, f, recv],
            device_id=device_at(target), device_id_type=MESH,
        )

    def own(src, dst, m, f):
        return pltpu.make_async_copy(src, dst, sem_local.at[m, f])

    def once(make):
        held = {}

        def get(m, f):
            if (m, f) not in held:
                held[m, f] = make(m, f)
            return held[m, f]

        return get

    @once
    def phase1(m, f):
        b = AXES[f][0]
        src = tokens.at[m, :, cols(m, f)]
        dst = tok_all.at[m, pos[b], :, cols(m, f)]
        far = [remote(src, dst, m, f, i, i, moved(pos, b, by)) for i, by in enumerate(RING)]
        return far, own(src, dst, m, f)

    def along_mid(m, f, base):
        a = AXES[f][1]

        def src(to):
            return stage.at[m, block(to, 160), cols(m, f)]

        dst = mid.at[m, block(pos[a], 160), cols(m, f)]
        far = [
            remote(src((pos[a] + by) % 4), dst, m, f, i, base + i, moved(pos, a, by)) for i, by in enumerate(RING)
        ]
        return far, own(src(pos[a]), dst, m, f)

    def along_last(m, f, base):
        a = AXES[f][2]

        def src(to, core):
            return stage.at[m, block(core * 4 + to, 80), cols(m, f)]

        dst = last.at[m, block(pos[3] * 4 + pos[a], 80), cols(m, f)]
        far = [
            remote(
                src((pos[a] + by) % 4, 1 - pos[3] if dc else pos[3]), dst, m, f, i, base + i, moved(pos, a, by, dc)
            )
            for i, (by, dc) in enumerate(LAST)
        ]
        return far, own(src(pos[a], pos[3]), dst, m, f)

    @once
    def phase2(m, f):
        return along_mid(m, f, 3)

    @once
    def phase3(m, f):
        return along_last(m, f, 6)

    @once
    def back3(m, f):
        return along_last(m, f, 13)

    @once
    def back2(m, f):
        return along_mid(m, f, 20)

    @once
    def back1(m, f):
        b = AXES[f][0]
        far = [
            remote(
                tok_all.at[m, (pos[b] + by) % 4, :, cols(m, f)], fin.at[m, i, :, cols(m, f)], m, f, i, 23 + i,
                moved(pos, b, by),
            )
            for i, by in enumerate(RING)
        ]
        return far, None

    def start(copies):
        far, near = copies
        for copy in far:
            copy.start()
        if near is not None:
            near.start()

    def arrive(copies):
        far, near = copies
        for copy in far:
            copy.wait_recv()
        if near is not None:
            near.wait()

    def sent(copies):
        for copy in copies[0]:
            copy.wait_send()

    tell = []
    for f in range(3):
        b = AXES[f][0]
        for i, by in enumerate(RING):
            tell.append(
                pltpu.make_async_remote_copy(
                    src_ref=info.at[f, pos[b]], dst_ref=info.at[f, pos[b]], send_sem=sem_info_s.at[f, i],
                    recv_sem=sem_info_r.at[f, i], device_id=device_at(moved(pos, b, by)), device_id_type=MESH,
                )
            )
    for copy in tell:
        copy.start()

    for m in range(batches):
        for f in range(3):
            start(phase1(m, f))
    loads = [
        pltpu.make_async_copy(src.at[0], dst, sem_w.at[i])
        for i, (src, dst) in enumerate(((w_gate, wg), (w_up, wu), (w_down, wd)))
    ]
    for copy in loads:
        copy.start()

    r = lax.broadcasted_iota(I32, (320, 320), 0)
    n = lax.broadcasted_iota(I32, (320, 320), 1)
    fifth = (r * 205) >> 10
    d0, d1, d2, d3 = fifth >> 4, (fifth >> 2) & 3, fifth & 3, r - fifth * 5
    swap[...] = jnp.where(n == d1 * 80 + d0 * 20 + d2 * 5 + d3, 1.0, 0.0).astype(BF)
    rot[...] = jnp.where(n == d2 * 80 + d0 * 20 + d1 * 5 + d3, 1.0, 0.0).astype(BF)
    rot_t[...] = jnp.where(n == d1 * 80 + d2 * 20 + d0 * 5 + d3, 1.0, 0.0).astype(BF)

    for copy in tell:
        copy.wait()

    def keys(m, f):
        low = jnp.maximum(info[f, 0, m, 0:8, :], info[f, 1, m, 0:8, :])
        high = jnp.maximum(info[f, 2, m, 0:8, :], info[f, 3, m, 0:8, :])
        return jnp.concatenate([low, high], axis=1)

    def weights(m, f):
        low = info[f, 0, m, 8:16, :] + info[f, 1, m, 8:16, :]
        high = info[f, 2, m, 8:16, :] + info[f, 3, m, 8:16, :]
        return jnp.concatenate([low, high], axis=1)

    def row_key(f, i):
        return (lax.broadcasted_iota(I32, (128, 256), 0) + (pos[AXES[f][0]] * 640 + i * 128)).astype(F32)

    def build_pick(m, f):
        key = keys(m, f)
        for i in range(5):
            row = row_key(f, i)
            hit = key[0:1, :] == row
            for k in range(1, 8):
                hit = hit | (key[k : k + 1, :] == row)
            pick[i * 128 : (i + 1) * 128, :] = jnp.where(hit, 1.0, 0.0).astype(BF)

    def build_comb(m, f):
        key = keys(m, f)
        gate = weights(m, f)
        for i in range(5):
            row = row_key(f, i)
            total = jnp.zeros((128, 256), F32)
            for k in range(8):
                total = jnp.where(key[k : k + 1, :] == row, gate[k : k + 1, :], total)
            comb[m, f, :, i * 128 : (i + 1) * 128] = total.T.astype(BF)

    def halves(work):
        def one(c, carry):
            work(c)
            return carry

        lax.fori_loop(0, 2, one, 0)

    def chunks(m, f):
        at = 0
        while at < widths[m][f]:
            size = min(512, widths[m][f] - at)
            yield starts[m][f] + at, size
            at += size

    def step1(m, f):
        build_pick(m, f)
        phase1(m, f)[1].wait()
        arrive((phase1(m, f)[0], None))
        for at, size in chunks(m, f):
            rows = tok_all[m, :, :, at : at + size].reshape(4 * rows_tok, size)
            stage[m, :, at : at + size] = dot(pick[...], rows).astype(BF)
        sent(phase1(m, f))
        start(phase2(m, f))

    def step2(m, f):
        arrive(phase2(m, f))
        sent(phase2(m, f))
        @halves
        def _(c):
            for at, size in chunks(m, f):
                rows = jnp.concatenate(
                    [mid[m, block(i * 2 + c, 80), at : at + size] for i in range(4)], axis=0
                )
                stage[m, block(c, 320), at : at + size] = dot(swap[...], rows).astype(BF)

        for by in RING:
            pl.semaphore_signal(
                free_mid.at[m, f], inc=1, device_id=device_at(moved(pos, AXES[f][1], by)), device_id_type=MESH
            )
        start(phase3(m, f))

    def side(copies, h):
        return [copy for copy, (by, dc) in zip(copies[0], LAST) if dc == h], None if h else copies[1]

    def half(h):
        return block(1 - pos[3] if h else pos[3], 320)

    def gather(m, f, h):
        arrive(side(phase3(m, f), h))
        if h == 0:
            sent(phase3(m, f))
        for at, size in chunks(m, f):
            rows = last[m, half(h), at : at + size]
            if f:
                rows = dot((rot, rot_t)[f - 1][...], rows).astype(BF)
            stage[m, half(h), at : at + size] = rows
        for by, dc in LAST:
            if dc == h:
                pl.semaphore_signal(
                    free_last.at[m, f, h], inc=1, device_id=device_at(moved(pos, AXES[f][2], by, dc)),
                    device_id_type=MESH,
                )

    def expand(m, h):
        def one(j, carry):
            at = pl.ds(pl.multiple_of(j * tile, tile), tile)
            rows = stage[m, half(h), :]
            gate = dot(rows, wg[:, at])
            up = dot(rows, wu[:, at])
            hidden[:, at] = (gate / (1.0 + jnp.exp(-gate)) * up).astype(BF)
            return carry

        lax.fori_loop(0, tiles, one, 0)

    def shrink(m, f, h):
        rows = hidden[...]
        if f:
            rows = dot((rot_t, rot)[f - 1][...], rows).astype(BF)
        for at, size in chunks(m, f):
            stage[m, half(h), at : at + size] = dot(rows, wd[:, at : at + size]).astype(BF)
        pl.semaphore_wait(free_last.at[m, f, h], 3 + h)
        start(side(back3(m, f), h))

    def step4(m, f):
        arrive(back3(m, f))
        sent(back3(m, f))
        @halves
        def _(c):
            for at, size in chunks(m, f):
                rows = dot(swap[...], last[m, block(c, 320), at : at + size]).astype(BF)
                for i in range(4):
                    stage[m, block(i * 2 + c, 80), at : at + size] = rows[i * 80 : i * 80 + 80, :]

        pl.semaphore_wait(free_mid.at[m, f], len(RING))
        start(back2(m, f))

    def step5(m, f):
        arrive(back2(m, f))
        sent(back2(m, f))
        for at, size in chunks(m, f):
            rows = dot(comb[m, f], mid[m, :, at : at + size]).astype(BF)
            tok_all[m, :, :, at : at + size] = rows.reshape(4, rows_tok, size)
        start(back1(m, f))

    @once
    def leave(m, f):
        return own(tok_all.at[m, pos[AXES[f][0]], :, cols(m, f)], out.at[m, :, cols(m, f)], m, f)

    def step6(m, f):
        arrive(back1(m, f))
        total = tok_all[m, pos[AXES[f][0]], :, cols(m, f)].astype(F32)
        for i in range(3):
            total = total + fin[m, i, :, cols(m, f)].astype(F32)
        tok_all[m, pos[AXES[f][0]], :, cols(m, f)] = total.astype(BF)
        leave(m, f).start()
        sent(back1(m, f))

    parts = range(3)
    for f in parts:
        step1(0, f)
    for f in parts:
        step1(1, f)
    for f in parts:
        build_comb(0, f)
    for f in parts:
        build_comb(1, f)
    for f in parts:
        step2(0, f)
    for f in parts:
        step2(1, f)
    for copy in loads:
        copy.wait()
    for f in parts:
        gather(0, f, 0)
    expand(0, 0)
    for f in parts:
        shrink(0, f, 0)
    for f in parts:
        gather(0, f, 1)
    expand(0, 1)
    for f in parts:
        shrink(0, f, 1)
    for f in parts:
        gather(1, f, 0)
    expand(1, 0)
    for f in parts:
        shrink(1, f, 0)
    for f in parts:
        gather(1, f, 1)
    expand(1, 1)
    for f in parts:
        shrink(1, f, 1)
    for f in parts:
        step4(0, f)
    for f in parts:
        step4(1, f)
    for f in parts:
        step5(0, f)
    for f in parts:
        step5(1, f)
    for f in parts:
        step6(0, f)
    for f in parts:
        step6(1, f)
    for f in parts:
        leave(0, f).wait()
    for f in parts:
        leave(1, f).wait()


def local(tokens, expert_ids, gate_weights, slot_expert, w_gate, w_up, w_down):
    batches, rows, width = tokens.shape
    ff = w_gate.shape[2]
    slots = 128 * CAP
    unit = width // 128
    thin = unit // 3 * 128
    widths = tuple((thin, width - 2 * thin, thin) if m % 2 else (thin, thin, width - 2 * thin) for m in range(batches))
    starts = tuple((0, w[0], w[0] + w[1]) for w in widths)
    tile = 256
    tiles = ff // tile

    vmem = pl.BlockSpec(memory_space=pltpu.VMEM)
    hbm = pl.BlockSpec(memory_space=pl.ANY)

    def body(*refs):
        kernel((starts, widths, tile, tiles), *refs)

    return pl.pallas_call(
        body,
        out_shape=jax.ShapeDtypeStruct(tokens.shape, BF),
        in_specs=[hbm, vmem, vmem, vmem, hbm, hbm, hbm],
        out_specs=hbm,
        scratch_shapes=[
            pltpu.VMEM((batches, 4, rows, width), BF),
            pltpu.VMEM((batches, slots, width), BF),
            pltpu.VMEM((batches, slots, width), BF),
            pltpu.VMEM((batches, slots, width), BF),
            pltpu.VMEM((batches, 3, rows, width), BF),
            pltpu.VMEM((3, 4, batches, 16, 128), F32),
            pltpu.VMEM((slots // 2, ff), BF),
            pltpu.VMEM((slots, 4 * rows), BF),
            pltpu.VMEM((batches, 3, 4 * rows, slots), BF),
            pltpu.VMEM((320, 320), BF),
            pltpu.VMEM((320, 320), BF),
            pltpu.VMEM((320, 320), BF),
            pltpu.VMEM((width, ff), BF),
            pltpu.VMEM((width, ff), BF),
            pltpu.VMEM((ff, width), BF),
            pltpu.SemaphoreType.DMA((batches, 3, 7)),
            pltpu.SemaphoreType.DMA((batches, 3, 26)),
            pltpu.SemaphoreType.DMA((batches, 3)),
            pltpu.SemaphoreType.DMA((3, 3)),
            pltpu.SemaphoreType.DMA((3, 3)),
            pltpu.SemaphoreType.DMA((3,)),
            pltpu.SemaphoreType.REGULAR((batches, 3)),
            pltpu.SemaphoreType.REGULAR((batches, 3, 2)),
        ],
        compiler_params=pltpu.CompilerParams(collective_id=0, has_side_effects=True, vmem_limit_bytes=62 << 20),
        cost_estimate=pl.CostEstimate(flops=60 * 10**9, bytes_accessed=24 * 10**6, transcendentals=10**6),
    )(tokens, jnp.swapaxes(expert_ids, 1, 2), jnp.swapaxes(gate_weights, 1, 2), slot_expert.reshape(1, -1), w_gate, w_up, w_down)


def solution(mesh):
    in_specs = (
        P(None, ("dp", "expert"), None),
        P(None, ("dp", "expert"), None),
        P(None, ("dp", "expert"), None),
        P(),
        P(("dp", "expert"), None, None),
        P(("dp", "expert"), None, None),
        P(("dp", "expert"), None, None),
    )
    out_specs = P(None, ("dp", "expert"), None)
    return jax.shard_map(local, mesh=mesh, in_specs=in_specs, out_specs=out_specs, check_vma=False)
```

```python
import jax
import jax.numpy as jnp
from jax import lax
from jax.experimental import pallas as pl
from jax.experimental.pallas import tpu as pltpu
from jax.sharding import PartitionSpec as P

MESH = pl.DeviceIdType.MESH
BF = jnp.bfloat16
F32 = jnp.float32
I32 = jnp.int32

AXES = ((0, 1, 2), (1, 2, 0), (2, 0, 1))
CAP = 5
RING = (1, 3, 2)
LAST = tuple((dl, dc) for dl in (1, 3, 2, 0) for dc in (0, 1) if (dl, dc) != (0, 0))


def dot(a, b):
    return jnp.dot(a, b, preferred_element_type=F32)


def device_at(pos):
    z, y, x, c = pos
    return (y // 2, ((z * 2 + y % 2) * 4 + x) * 2 + c)


def moved(pos, axis, by, core=0):
    out = list(pos)
    out[axis] = (pos[axis] + by) % 4
    if core:
        out[3] = 1 - pos[3]
    return tuple(out)


def kernel(
    sizes, tokens, ids, gates, slots, w_gate, w_up, w_down, out,
    tok_all, stage, mid, last, fin, info, hidden, pick, comb, swap, rot, rot_t,
    wg, wu, wd, sem_send, sem_recv, sem_local, sem_info_s, sem_info_r, sem_w, free_mid, free_last,
):
    batches, rows_tok, _ = tokens.shape
    starts, widths, tile, tiles = sizes
    dp = lax.axis_index("dp")
    ex = lax.axis_index("expert")
    pos = (ex // 16, dp * 2 + (ex // 8) % 2, (ex // 2) % 4, ex % 2)

    def cols(m, f):
        return pl.ds(starts[m][f], widths[m][f])

    def block(i, n):
        return pl.ds(pl.multiple_of(i * n, n), n)

    peers = [(a, by, c) for a in range(3) for by in (1, 2, 3) for c in (0, 1)] + [(0, 0, 1)]
    barrier = pltpu.get_barrier_semaphore()
    for a, by, c in peers:
        pl.semaphore_signal(barrier, inc=1, device_id=device_at(moved(pos, a, by, c)), device_id_type=MESH)
    sub = lax.broadcasted_iota(I32, (128, 128), 0)
    lane = lax.broadcasted_iota(I32, (128, 128), 1)
    holder = jnp.sum(jnp.where(slots[...] == sub, lane, 0).astype(F32), axis=1, keepdims=True) * 8.0
    before = jnp.where((sub < 64) & (sub < lane % 64), 1.0, 0.0).astype(BF)
    lane8 = lax.broadcasted_iota(I32, (8, 128), 1)
    twice = jnp.where(sub[:64] == lane[:64] % 64, 1.0, 0.0).astype(BF)

    for m in range(batches):
        names = dot(ids[m].astype(F32).astype(BF), twice).astype(I32)
        gate_rows = dot(gates[m].astype(BF), twice)
        same = [names[k : k + 1, :] == sub for k in range(8)]
        chosen = jnp.where(same[0], 1.0, 0.0)
        for k in range(1, 8):
            chosen = chosen + jnp.where(same[k], 1.0, 0.0)
        value = dot(chosen.astype(BF), before) + holder
        found = jnp.concatenate(
            [jnp.sum(jnp.where(same[k], value, 0.0), axis=0, keepdims=True) for k in range(8)], axis=0
        ).astype(I32)
        rank = found & 7
        where = found >> 3
        at = (
            (where >> 4) & 3,
            ((where >> 3) & 1) + ((where >> 6) & 1) * 2,
            (where >> 1) & 3,
            where & 1,
        )
        for f in range(3):
            b, a, l = AXES[f]
            key = at[b] * 640 + at[a] * 160 + (at[3] * 4 + at[l]) * 20 + pos[b] * CAP + rank
            mine = (lane8 >= 64) == (lax.broadcast(pos[b] % 2, (8, 128)) == 1)
            info[f, pos[b], m, 0:8, :] = jnp.where(mine, key.astype(F32), -1.0)
            info[f, pos[b], m, 8:16, :] = jnp.where(mine, gate_rows, 0.0)
    pl.semaphore_wait(barrier, len(peers))

    def remote(src, dst, m, f, send, recv, target):
        return pltpu.make_async_remote_copy(
            src_ref=src, dst_ref=dst, send_sem=sem_send.at[m, f, send], recv_sem=sem_recv.at[m, f, recv],
            device_id=device_at(target), device_id_type=MESH,
        )

    def own(src, dst, m, f):
        return pltpu.make_async_copy(src, dst, sem_local.at[m, f])

    def once(make):
        held = {}

        def get(m, f):
            if (m, f) not in held:
                held[m, f] = make(m, f)
            return held[m, f]

        return get

    @once
    def phase1(m, f):
        b = AXES[f][0]
        src = tokens.at[m, :, cols(m, f)]
        dst = tok_all.at[m, pos[b], :, cols(m, f)]
        far = [remote(src, dst, m, f, 3 + i, i, moved(pos, b, by)) for i, by in enumerate(RING)]
        return far, own(src, dst, m, f)

    def along_mid(m, f, base):
        a = AXES[f][1]

        def src(to):
            return stage.at[m, block(to, 160), cols(m, f)]

        dst = mid.at[m, block(pos[a], 160), cols(m, f)]
        far = [
            remote(src((pos[a] + by) % 4), dst, m, f, i, base + i, moved(pos, a, by)) for i, by in enumerate(RING)
        ]
        return far, own(src(pos[a]), dst, m, f)

    def along_last(m, f, base):
        a = AXES[f][2]

        def src(to, core):
            return stage.at[m, block(core * 4 + to, 80), cols(m, f)]

        dst = last.at[m, block(pos[3] * 4 + pos[a], 80), cols(m, f)]
        far = [
            remote(
                src((pos[a] + by) % 4, 1 - pos[3] if dc else pos[3]), dst, m, f, i, base + i, moved(pos, a, by, dc)
            )
            for i, (by, dc) in enumerate(LAST)
        ]
        return far, own(src(pos[a], pos[3]), dst, m, f)

    @once
    def phase2(m, f):
        return along_mid(m, f, 3)

    @once
    def phase3(m, f):
        return along_last(m, f, 6)

    @once
    def back3(m, f):
        return along_last(m, f, 13)

    @once
    def back2(m, f):
        return along_mid(m, f, 20)

    @once
    def back1(m, f):
        b = AXES[f][0]
        far = [
            remote(
                tok_all.at[m, (pos[b] + by) % 4, :, cols(m, f)], fin.at[m, i, :, cols(m, f)], m, f, 3 + i, 23 + i,
                moved(pos, b, by),
            )
            for i, by in enumerate(RING)
        ]
        return far, None

    def start(copies):
        far, near = copies
        for copy in far:
            copy.start()
        if near is not None:
            near.start()

    def arrive(copies):
        far, near = copies
        for copy in far:
            copy.wait_recv()
        if near is not None:
            near.wait()

    def sent(copies):
        for copy in copies[0]:
            copy.wait_send()

    tell = []
    for f in range(3):
        b = AXES[f][0]
        for i, by in enumerate(RING):
            tell.append(
                pltpu.make_async_remote_copy(
                    src_ref=info.at[f, pos[b]], dst_ref=info.at[f, pos[b]], send_sem=sem_info_s.at[f, i],
                    recv_sem=sem_info_r.at[f, i], device_id=device_at(moved(pos, b, by)), device_id_type=MESH,
                )
            )
    for copy in tell:
        copy.start()

    for m in range(batches):
        for f in range(3):
            start(phase1(m, f))
    loads = [
        pltpu.make_async_copy(src.at[0], dst, sem_w.at[i])
        for i, (src, dst) in enumerate(((w_gate, wg), (w_up, wu), (w_down, wd)))
    ]
    for copy in loads:
        copy.start()

    r = lax.broadcasted_iota(I32, (320, 320), 0)
    n = lax.broadcasted_iota(I32, (320, 320), 1)
    fifth = (r * 205) >> 10
    d0, d1, d2, d3 = fifth >> 4, (fifth >> 2) & 3, fifth & 3, r - fifth * 5
    swap[...] = jnp.where(n == d1 * 80 + d0 * 20 + d2 * 5 + d3, 1.0, 0.0).astype(BF)
    rot[...] = jnp.where(n == d2 * 80 + d0 * 20 + d1 * 5 + d3, 1.0, 0.0).astype(BF)
    rot_t[...] = jnp.where(n == d1 * 80 + d2 * 20 + d0 * 5 + d3, 1.0, 0.0).astype(BF)

    for copy in tell:
        copy.wait()

    def keys(m, f):
        low = jnp.maximum(info[f, 0, m, 0:8, :], info[f, 1, m, 0:8, :])
        high = jnp.maximum(info[f, 2, m, 0:8, :], info[f, 3, m, 0:8, :])
        return jnp.concatenate([low, high], axis=1)

    def weights(m, f):
        low = info[f, 0, m, 8:16, :] + info[f, 1, m, 8:16, :]
        high = info[f, 2, m, 8:16, :] + info[f, 3, m, 8:16, :]
        return jnp.concatenate([low, high], axis=1)

    def row_key(f, i):
        return (lax.broadcasted_iota(I32, (128, 256), 0) + (pos[AXES[f][0]] * 640 + i * 128)).astype(F32)

    def build_pick(m, f):
        key = keys(m, f)
        for i in range(5):
            row = row_key(f, i)
            hit = key[0:1, :] == row
            for k in range(1, 8):
                hit = hit | (key[k : k + 1, :] == row)
            pick[i * 128 : (i + 1) * 128, :] = jnp.where(hit, 1.0, 0.0).astype(BF)

    def build_comb(m, f):
        key = keys(m, f)
        gate = weights(m, f)
        for i in range(5):
            row = row_key(f, i)
            total = jnp.zeros((128, 256), F32)
            for k in range(8):
                total = jnp.where(key[k : k + 1, :] == row, gate[k : k + 1, :], total)
            comb[m, f, :, i * 128 : (i + 1) * 128] = total.T.astype(BF)

    def halves(work):
        def one(c, carry):
            work(c)
            return carry

        lax.fori_loop(0, 2, one, 0)

    def chunks(m, f):
        at = 0
        while at < widths[m][f]:
            size = min(512, widths[m][f] - at)
            yield starts[m][f] + at, size
            at += size

    def step1(m, f):
        build_pick(m, f)
        phase1(m, f)[1].wait()
        arrive((phase1(m, f)[0], None))
        for at, size in chunks(m, f):
            rows = tok_all[m, :, :, at : at + size].reshape(4 * rows_tok, size)
            stage[m, :, at : at + size] = dot(pick[...], rows).astype(BF)
        start(phase2(m, f))

    def step2(m, f):
        arrive(phase2(m, f))
        sent(phase1(m, f))
        sent(phase2(m, f))
        @halves
        def _(c):
            for at, size in chunks(m, f):
                rows = jnp.concatenate(
                    [mid[m, block(i * 2 + c, 80), at : at + size] for i in range(4)], axis=0
                )
                stage[m, block(c, 320), at : at + size] = dot(swap[...], rows).astype(BF)

        for by in RING:
            pl.semaphore_signal(
                free_mid.at[m, f], inc=1, device_id=device_at(moved(pos, AXES[f][1], by)), device_id_type=MESH
            )
        start(phase3(m, f))

    def side(copies, h):
        return [copy for copy, (by, dc) in zip(copies[0], LAST) if dc == h], None if h else copies[1]

    def half(h):
        return block(1 - pos[3] if h else pos[3], 320)

    def gather(m, f, h):
        arrive(side(phase3(m, f), h))
        if h == 0:
            sent(phase3(m, f))
        for at, size in chunks(m, f):
            rows = last[m, half(h), at : at + size]
            if f:
                rows = dot((rot, rot_t)[f - 1][...], rows).astype(BF)
            stage[m, half(h), at : at + size] = rows
        for by, dc in LAST:
            if dc == h:
                pl.semaphore_signal(
                    free_last.at[m, f, h], inc=1, device_id=device_at(moved(pos, AXES[f][2], by, dc)),
                    device_id_type=MESH,
                )

    def expand(m, h):
        def one(j, carry):
            at = pl.ds(pl.multiple_of(j * tile, tile), tile)
            rows = stage[m, half(h), :]
            gate = dot(rows, wg[:, at])
            up = dot(rows, wu[:, at])
            hidden[:, at] = (gate / (1.0 + jnp.exp(-gate)) * up).astype(BF)
            return carry

        lax.fori_loop(0, tiles, one, 0)

    def shrink(m, f, h):
        rows = hidden[...]
        if f:
            rows = dot((rot_t, rot)[f - 1][...], rows).astype(BF)
        for at, size in chunks(m, f):
            stage[m, half(h), at : at + size] = dot(rows, wd[:, at : at + size]).astype(BF)
        pl.semaphore_wait(free_last.at[m, f, h], 3 + h)
        start(side(back3(m, f), h))

    def step4(m, f):
        arrive(back3(m, f))
        sent(back3(m, f))
        @halves
        def _(c):
            for at, size in chunks(m, f):
                rows = dot(swap[...], last[m, block(c, 320), at : at + size]).astype(BF)
                for i in range(4):
                    stage[m, block(i * 2 + c, 80), at : at + size] = rows[i * 80 : i * 80 + 80, :]

        pl.semaphore_wait(free_mid.at[m, f], len(RING))
        start(back2(m, f))

    def step5(m, f):
        arrive(back2(m, f))
        for at, size in chunks(m, f):
            rows = dot(comb[m, f], mid[m, :, at : at + size]).astype(BF)
            tok_all[m, :, :, at : at + size] = rows.reshape(4, rows_tok, size)
        start(back1(m, f))

    @once
    def leave(m, f):
        return own(tok_all.at[m, pos[AXES[f][0]], :, cols(m, f)], out.at[m, :, cols(m, f)], m, f)

    def step6(m, f):
        arrive(back1(m, f))
        total = tok_all[m, pos[AXES[f][0]], :, cols(m, f)].astype(F32)
        for i in range(3):
            total = total + fin[m, i, :, cols(m, f)].astype(F32)
        tok_all[m, pos[AXES[f][0]], :, cols(m, f)] = total.astype(BF)
        leave(m, f).start()
        sent(back2(m, f))
        sent(back1(m, f))

    parts = range(3)
    for f in parts:
        step1(0, f)
    for f in parts:
        step1(1, f)
    for f in parts:
        build_comb(0, f)
    for f in parts:
        step2(0, f)
    for f in parts:
        step2(1, f)
    for f in parts:
        build_comb(1, f)
    for copy in loads:
        copy.wait()
    for f in parts:
        gather(0, f, 0)
    expand(0, 0)
    for f in parts:
        shrink(0, f, 0)
    for f in parts:
        gather(0, f, 1)
    expand(0, 1)
    for f in parts:
        shrink(0, f, 1)
    for f in parts:
        gather(1, f, 0)
    expand(1, 0)
    for f in parts:
        shrink(1, f, 0)
    for f in parts:
        gather(1, f, 1)
    expand(1, 1)
    for f in parts:
        shrink(1, f, 1)
    for f in parts:
        step4(0, f)
    for f in parts:
        step4(1, f)
    for f in parts:
        step5(0, f)
    for f in parts:
        step5(1, f)
    for f in parts:
        step6(0, f)
    for f in parts:
        step6(1, f)
    for f in parts:
        leave(0, f).wait()
    for f in parts:
        leave(1, f).wait()


def local(tokens, expert_ids, gate_weights, slot_expert, w_gate, w_up, w_down):
    batches, rows, width = tokens.shape
    ff = w_gate.shape[2]
    slots = 128 * CAP
    unit = width // 128
    thin = unit // 3 * 128
    widths = tuple((thin, width - 2 * thin, thin) if m % 2 else (thin, thin, width - 2 * thin) for m in range(batches))
    starts = tuple((0, w[0], w[0] + w[1]) for w in widths)
    tile = 256
    tiles = ff // tile

    vmem = pl.BlockSpec(memory_space=pltpu.VMEM)
    hbm = pl.BlockSpec(memory_space=pl.ANY)

    def body(*refs):
        kernel((starts, widths, tile, tiles), *refs)

    return pl.pallas_call(
        body,
        out_shape=jax.ShapeDtypeStruct(tokens.shape, BF),
        in_specs=[hbm, vmem, vmem, vmem, hbm, hbm, hbm],
        out_specs=hbm,
        scratch_shapes=[
            pltpu.VMEM((batches, 4, rows, width), BF),
            pltpu.VMEM((batches, slots, width), BF),
            pltpu.VMEM((batches, slots, width), BF),
            pltpu.VMEM((batches, slots, width), BF),
            pltpu.VMEM((batches, 3, rows, width), BF),
            pltpu.VMEM((3, 4, batches, 16, 128), F32),
            pltpu.VMEM((slots // 2, ff), BF),
            pltpu.VMEM((slots, 4 * rows), BF),
            pltpu.VMEM((batches, 3, 4 * rows, slots), BF),
            pltpu.VMEM((320, 320), BF),
            pltpu.VMEM((320, 320), BF),
            pltpu.VMEM((320, 320), BF),
            pltpu.VMEM((width, ff), BF),
            pltpu.VMEM((width, ff), BF),
            pltpu.VMEM((ff, width), BF),
            pltpu.SemaphoreType.DMA((batches, 3, 7)),
            pltpu.SemaphoreType.DMA((batches, 3, 26)),
            pltpu.SemaphoreType.DMA((batches, 3)),
            pltpu.SemaphoreType.DMA((3, 3)),
            pltpu.SemaphoreType.DMA((3, 3)),
            pltpu.SemaphoreType.DMA((3,)),
            pltpu.SemaphoreType.REGULAR((batches, 3)),
            pltpu.SemaphoreType.REGULAR((batches, 3, 2)),
        ],
        compiler_params=pltpu.CompilerParams(collective_id=0, has_side_effects=True, vmem_limit_bytes=62 << 20),
        cost_estimate=pl.CostEstimate(flops=60 * 10**9, bytes_accessed=24 * 10**6, transcendentals=10**6),
    )(tokens, jnp.swapaxes(expert_ids, 1, 2), jnp.swapaxes(gate_weights, 1, 2), slot_expert.reshape(1, -1), w_gate, w_up, w_down)


def solution(mesh):
    in_specs = (
        P(None, ("dp", "expert"), None),
        P(None, ("dp", "expert"), None),
        P(None, ("dp", "expert"), None),
        P(),
        P(("dp", "expert"), None, None),
        P(("dp", "expert"), None, None),
        P(("dp", "expert"), None, None),
    )
    out_specs = P(None, ("dp", "expert"), None)
    return jax.shard_map(local, mesh=mesh, in_specs=in_specs, out_specs=out_specs, check_vma=False)
```
